256 devices in a mesh: section: 8 (over z), blk: 32 (over y, x, core).
Axes of the slice: x: 4, y: 4, z: 8, core: 2. Of those that a mesh axis runs over, the one named last changes fastest.
Arguments:
- raw: bfloat16 [8, 4096, 8192], P('section', 'blk'), may hold values from -6 to 6
- pair_blocks: int32 [32, 2], replicated, may hold values from 0 to 31
Outputs:
- stacked: float32 [32, 128, 1024], P('blk', 'section')
The draws below stay inside these ranges and needn't reach their ends.
All inputs are finite; a program needn't handle non-finite values.
Results may differ from the reference program's by a relative error of at most 0.0029.
Values may be sent and summed in bfloat16 or wider, within the bound.
No kernel may reach another device: no remote copies, remote signals or barrier semaphores. Data moves between devices by JAX's collectives and lax.ppermute only.
A program may use at most 128 MiB of HBM per device.

```python
import math
import jax
import jax.numpy as jnp
from jax import lax

NF = 8192
CB = 128
LAGS = 1024
SEGS = 8
NBLOCKS = 32
CHANNELS = 4096
PAIRS = 32


def set_ends(array, key, least, top_value):
    longest = array.shape.index(max(array.shape))
    spots = []
    for shift in (0, 1):
        where = [jax.random.randint(jax.random.fold_in(key, axis), (), 0, length) for axis, length in enumerate(array.shape)]
        where[longest] = (where[longest] + shift) % array.shape[longest]
        spots.append(tuple(where))
    return array.at[spots[0]].set(least).at[spots[1]].set(top_value)


def steps_of(rng, shape, shards, smallest, top_value):
    loudness = 1.0
    for position, blocks in shards:
        heights = jax.random.uniform(jax.random.fold_in(jax.random.fold_in(rng, 6), position), (blocks,), jnp.float32, smallest / len(shards), top_value / len(shards))
        loudness = loudness * jnp.repeat(jnp.exp(heights), shape[position] // blocks).reshape((-1,) + (1,) * (len(shape) - 1 - position))
    return loudness


def centred(rng, shape, scale, bound, cuts=(), kind=jnp.bfloat16):
    entries = jax.random.normal(rng, shape, jnp.float32) * scale
    if len(cuts) > 0:
        entries = steps_of(rng, shape, cuts, -0.22, 0.18) * entries
    return jnp.clip(entries, min=-bound, max=bound).astype(kind)


def setup_inputs(seed: int = 0) -> dict:
    streams_of = jax.random.split(jax.random.key(seed), 3)
    raw = centred(streams_of[0], (SEGS, CHANNELS, NF), 1.0, 6.0, ((0, 8), (1, 32)))
    pair_blocks = set_ends(jax.random.randint(streams_of[1], (PAIRS, 2), 0, NBLOCKS), jax.random.fold_in(streams_of[1], 1), 0, NBLOCKS - 1).astype(jnp.int32)
    return {"raw": raw, "pair_blocks": pair_blocks}


def whiten(segment):
    x = segment.astype(jnp.float32)
    x = x - lax.optimization_barrier(jnp.mean(x, axis=-1, keepdims=True))
    spectrum = jnp.fft.fft(x, axis=-1)
    real_part = jnp.real(spectrum).astype(jnp.float32)
    imag_part = jnp.imag(spectrum).astype(jnp.float32)
    power = real_part * real_part + imag_part * imag_part
    level = lax.optimization_barrier(jnp.mean(power, axis=-1, keepdims=True))
    scale = lax.rsqrt(power + 0.1 * level + 1e-06)
    return ((real_part * scale).astype(jnp.bfloat16), (imag_part * scale).astype(jnp.bfloat16))

def lag_tables():
    bins = jnp.arange(NF, dtype=jnp.int32)
    shifts = (jnp.arange(LAGS, dtype=jnp.int32) - LAGS // 2) % NF
    phase = bins[:, None] * shifts[None, :] % NF
    angle = phase.astype(jnp.float32) * jnp.float32(2.0 * math.pi / NF)
    cosine = jnp.cos(angle).astype(jnp.bfloat16).astype(jnp.float32)
    sine = jnp.sin(angle).astype(jnp.bfloat16).astype(jnp.float32)
    return (cosine, sine)

def reference(raw, pair_blocks):
    source = pair_blocks[:, 0].astype(jnp.int32)
    target = pair_blocks[:, 1].astype(jnp.int32)

    def add_segment(carry, segment):
        real_part, imag_part = whiten(segment)
        real_part = real_part.reshape(NBLOCKS, CB, NF).astype(jnp.float32)
        imag_part = imag_part.reshape(NBLOCKS, CB, NF).astype(jnp.float32)
        ar, ai = (real_part[source], imag_part[source])
        br, bi = (real_part[target], imag_part[target])
        cross_real = (ar * br + ai * bi).astype(jnp.bfloat16).astype(jnp.float32)
        cross_imag = (ai * br - ar * bi).astype(jnp.bfloat16).astype(jnp.float32)
        return ((carry[0] + cross_real, carry[1] + cross_imag), None)
    start = (jnp.zeros((PAIRS, CB, NF), jnp.float32), jnp.zeros((PAIRS, CB, NF), jnp.float32))
    (sum_real, sum_imag), unused = lax.scan(add_segment, start, raw)
    cosine, sine = lag_tables()
    high = lax.Precision.HIGHEST
    lagged = jnp.dot(sum_real.reshape(PAIRS * CB, NF), cosine, precision=high, preferred_element_type=jnp.float32)
    lagged = lagged - jnp.dot(sum_imag.reshape(PAIRS * CB, NF), sine, precision=high, preferred_element_type=jnp.float32)
    lagged = lagged * jnp.float32(NF ** (-0.5))
    return lagged.reshape(PAIRS, CB, LAGS)
```

```python
import math

import jax
import jax.numpy as jnp
import ml_dtypes
import numpy as np
from jax import lax
from jax.experimental import pallas as pl
from jax.experimental.pallas import tpu as pltpu
from jax.sharding import PartitionSpec as P

NF = 8192
LAGS = 1024
LANES = 128
ROWS = 16
SLOTS = 32
HALF = math.sqrt(0.5)
AXES = ("section", "blk")
RESIDUES = (
    [8, 16, 24]
    + [4 + 8 * r for r in range(4)]
    + [q + 8 * r for q in (1, 2, 3) for r in range(8)]
)


def bin_numbers():
    lane = np.arange(LANES)
    first = np.where(lane < 64, 64 * (lane + 1), 32 + 64 * (lane - 64))
    return np.stack([first] + [r + 64 * lane for r in RESIDUES])


def twiddles():
    lane = np.arange(LANES)
    turns = [lane / 128.0, lane / 256.0 + lane / 2.0] + [lane * r / NF for r in RESIDUES]
    angle = 2.0 * np.pi * np.stack(turns)
    return np.stack([np.cos(angle), np.sin(angle)]).astype(np.float32)


def last_transform():
    index = np.arange(LANES)
    angle = 2.0 * np.pi * (index[:, None] * index[None, :] % LANES) / LANES
    cosine, sine = np.cos(angle), np.sin(angle)
    full = np.block([[cosine, -sine], [sine, cosine]])
    high = full.astype(ml_dtypes.bfloat16)
    low = (full - high.astype(np.float64)).astype(ml_dtypes.bfloat16)
    return np.stack([high, low])


def lag_table():
    bins = bin_numbers()
    shifts = (np.arange(LAGS) - LAGS // 2) % NF
    angle = 2.0 * np.pi * (bins.reshape(-1)[:, None] * shifts[None, :] % NF) / NF
    weight = np.where(bins.reshape(-1) == NF // 2, 0.5, 1.0)[:, None]
    cosine = np.cos(angle).astype(ml_dtypes.bfloat16).astype(np.float32) * weight
    sine = np.sin(angle).astype(ml_dtypes.bfloat16).astype(np.float32) * weight
    return np.concatenate([cosine, -sine]).astype(ml_dtypes.bfloat16)


def real8(x):
    s0, d0, s2, d2 = x[0] + x[4], x[0] - x[4], x[2] + x[6], x[2] - x[6]
    s1, d1, s3, d3 = x[1] + x[5], x[1] - x[5], x[3] + x[7], x[3] - x[7]
    even, odd = s0 + s2, s1 + s3
    u, v = (d1 - d3) * HALF, (d1 + d3) * HALF
    return [
        (even + odd, None),
        (d0 + u, -(d2 + v)),
        (s0 - s2, s3 - s1),
        (d0 - u, d2 - v),
        (even - odd, None),
    ]


def complex8(re, im):
    def add(i, j):
        return (i[0] + j[0], i[1] + j[1])

    def sub(i, j):
        return (i[0] - j[0], i[1] - j[1])

    def sub_i(i, j):
        return (i[0] + j[1], i[1] - j[0])

    def add_i(i, j):
        return (i[0] - j[1], i[1] + j[0])

    t = list(zip(re, im))
    a0, a1, a2, a3 = add(t[0], t[4]), sub(t[0], t[4]), add(t[2], t[6]), sub(t[2], t[6])
    a4, a5, a6, a7 = add(t[1], t[5]), sub(t[1], t[5]), add(t[3], t[7]), sub(t[3], t[7])
    b0, b2, b1, b3 = add(a0, a2), sub(a0, a2), sub_i(a1, a3), add_i(a1, a3)
    b4, b6, b5, b7 = add(a4, a6), sub(a4, a6), sub_i(a5, a7), add_i(a5, a7)
    c5 = ((b5[0] + b5[1]) * HALF, (b5[1] - b5[0]) * HALF)
    c7 = ((b7[1] - b7[0]) * HALF, (b7[0] + b7[1]) * -HALF)
    return [
        add(b0, b4), add(b1, c5), sub_i(b2, b6), add(b3, c7),
        sub(b0, b4), sub(b1, c5), add_i(b2, b6), sub(b3, c7),
    ]


def whiten_kernel(raw_ref, twist_ref, last_ref, out_ref, part_ref, high_ref, low_ref, spec_ref, turn_ref):
    f32, bf16 = jnp.float32, jnp.bfloat16

    def put(slot, re, im):
        cosine, sine = twist_ref[0, slot : slot + 1, :], twist_ref[1, slot : slot + 1, :]
        if im is None:
            zr, zi = re * cosine, re * -sine
        else:
            zr, zi = re * cosine + im * sine, im * cosine - re * sine
        rows = pl.ds(slot * ROWS, ROWS)
        for z, lanes in ((zr, pl.ds(0, LANES)), (zi, pl.ds(LANES, LANES))):
            high = z.astype(bf16)
            high_ref[rows, lanes] = high
            low_ref[rows, lanes] = (z - high.astype(f32)).astype(bf16)

    for b in range(8):
        x = [raw_ref[0, :, pl.ds((8 * a + b) * LANES, LANES)].astype(f32) for a in range(8)]
        y = real8(x)
        for q in range(5):
            part_ref[0, q, b] = y[q][0]
            if y[q][1] is not None:
                part_ref[1, q, b] = y[q][1]
    whole = real8([part_ref[0, 0, b] for b in range(8)])
    zero = whole[0][0] - jnp.mean(whole[0][0], axis=-1, keepdims=True)
    put(0, zero, None)
    put(1, whole[4][0], None)
    for r in (1, 2, 3):
        put(1 + r, *whole[r])
    slot = 5
    for q in (4, 1, 2, 3):
        re, im = [], []
        for b in range(8):
            cosine, sine = math.cos(2 * math.pi * b * q / 64), math.sin(2 * math.pi * b * q / 64)
            yr = part_ref[0, q, b]
            if q == 4:
                re.append(yr * cosine if b else yr)
                im.append(yr * -sine if b else jnp.zeros_like(yr))
            else:
                yi = part_ref[1, q, b]
                re.append(yr * cosine + yi * sine if b else yr)
                im.append(yi * cosine - yr * sine if b else yi)
        z = complex8(re, im)
        for r in range(4 if q == 4 else 8):
            put(slot, *z[r])
            slot += 1

    high, low = high_ref[...], low_ref[...]
    spec = jnp.dot(high, last_ref[0], preferred_element_type=f32)
    spec = spec + jnp.dot(high, last_ref[1], preferred_element_type=f32)
    spec = spec + jnp.dot(low, last_ref[0], preferred_element_type=f32)
    spec_ref[...] = spec

    lane = lax.broadcasted_iota(jnp.int32, (ROWS, LANES), 1)

    def get(slot):
        re = spec_ref[pl.ds((slot + 1) * ROWS, ROWS), pl.ds(0, LANES)]
        im = spec_ref[pl.ds((slot + 1) * ROWS, ROWS), pl.ds(LANES, LANES)]
        if slot == 0:
            re = jnp.where(lane < 64, spec_ref[pl.ds(0, ROWS), pl.ds(0, LANES)], re)
            im = jnp.where(lane < 64, spec_ref[pl.ds(0, ROWS), pl.ds(LANES, LANES)], im)
        return re, im

    total = None
    for slot in range(SLOTS):
        re, im = get(slot)
        power = re * re + im * im
        if slot == 0:
            power = jnp.where(lane == 63, power * 0.5, power)
        total = power if total is None else total + power
    level = jnp.sum(total, axis=-1, keepdims=True) * (2.0 / NF)
    floor = jnp.broadcast_to(0.1 * level + 1e-06, (ROWS, LANES))
    for slot in range(SLOTS):
        re, im = get(slot)
        scale = lax.rsqrt(re * re + im * im + floor)
        turn_ref[pl.ds(slot, ROWS, stride=2 * SLOTS), :] = re * scale
        turn_ref[pl.ds(slot + SLOTS, ROWS, stride=2 * SLOTS), :] = im * scale
    out_ref[0, :, 0, 0] = turn_ref[...].astype(bf16).reshape(ROWS, 2 * SLOTS, LANES)


def whiten(raw):
    steps = raw.shape[1] // ROWS
    return pl.pallas_call(
        whiten_kernel,
        grid=(steps,),
        out_shape=jax.ShapeDtypeStruct((2, ROWS, 2, 2, 2 * SLOTS, LANES), jnp.bfloat16),
        in_specs=[
            pl.BlockSpec((1, ROWS, NF), lambda g: (0, g, 0)),
            pl.BlockSpec((2, SLOTS + 1, LANES), lambda g: (0, 0, 0)),
            pl.BlockSpec((2, 2 * LANES, 2 * LANES), lambda g: (0, 0, 0)),
        ],
        out_specs=pl.BlockSpec(
            (1, ROWS, 1, 1, 2 * SLOTS, LANES), lambda g: (g % 2, 0, g // 4, (g // 2) % 2, 0, 0)
        ),
        scratch_shapes=[
            pltpu.VMEM((2, 5, 8, ROWS, LANES), jnp.float32),
            pltpu.VMEM(((SLOTS + 1) * ROWS, 2 * LANES), jnp.bfloat16),
            pltpu.VMEM(((SLOTS + 1) * ROWS, 2 * LANES), jnp.bfloat16),
            pltpu.VMEM(((SLOTS + 1) * ROWS, 2 * LANES), jnp.float32),
            pltpu.VMEM((ROWS * 2 * SLOTS, LANES), jnp.float32),
        ],
        compiler_params=pltpu.CompilerParams(vmem_limit_bytes=32 * 2**20),
        name="whiten",
    )(raw, jnp.asarray(twiddles()), jnp.asarray(last_transform()))


def lag_kernel(pairs_ref, spec_ref, table_ref, keep_ref, send_ref, cross_ref, left_ref, turn_ref):
    f32, bf16 = jnp.float32, jnp.bfloat16

    def one(i, carry):
        first, second = pairs_ref[0, i], pairs_ref[1, i]
        for h in range(2):
            for j in range(2):
                a = spec_ref[h * 32 + first, j].astype(f32)
                b = spec_ref[h * 32 + second, j].astype(f32)
                ar, ai, br, bi = a[:SLOTS], a[SLOTS:], b[:SLOTS], b[SLOTS:]
                row = pl.multiple_of(((h * 2 + j) * 32 + i) * 2 * SLOTS, 2 * SLOTS)
                cross_ref[pl.ds(row, SLOTS), :] = ar * br + ai * bi
                cross_ref[pl.ds(row + SLOTS, SLOTS), :] = ai * br - ar * bi
        return carry

    lax.fori_loop(0, 32, one, 0)
    for slot in range(2 * SLOTS):
        left_ref[:, pl.ds(slot * LANES, LANES)] = cross_ref[pl.ds(slot, 128, stride=2 * SLOTS), :].astype(bf16)
    lags = jnp.dot(left_ref[...], table_ref[...], preferred_element_type=f32)
    lags = (lags[:64] + lags[64:]) * (2.0 * NF**-0.5)
    for q in range(8):
        turn_ref[pl.ds(q, 64, stride=8), :] = lags[:, q * LANES : (q + 1) * LANES]
    turned = turn_ref[...].reshape(2, 2, 16, 8, LANES)
    keep_ref[...] = turned[:, 0].astype(bf16)
    send_ref[...] = turned[:, 1].astype(bf16)


def correlate(pairs, spectra):
    half = jax.ShapeDtypeStruct((2, 16, 8, LANES), jnp.bfloat16)
    vmem = pl.BlockSpec(memory_space=pltpu.VMEM)
    return pl.pallas_call(
        lag_kernel,
        out_shape=(half, half),
        in_specs=[pl.BlockSpec(memory_space=pltpu.SMEM), vmem, vmem],
        out_specs=(vmem, vmem),
        scratch_shapes=[
            pltpu.VMEM((128 * 2 * SLOTS, LANES), jnp.float32),
            pltpu.VMEM((128, NF), jnp.bfloat16),
            pltpu.VMEM((64 * 8, LANES), jnp.float32),
        ],
        compiler_params=pltpu.CompilerParams(vmem_limit_bytes=48 * 2**20),
        name="correlate",
    )(pairs, spectra, jnp.asarray(lag_table()))


def stack_kernel(lags_ref, out_ref, turn_ref):
    total = lags_ref[0].astype(jnp.float32)
    for t in range(1, 4):
        total = total + lags_ref[t].astype(jnp.float32)
    turn_ref[...] = total.reshape(16 * 8, LANES)
    for q in range(8):
        out_ref[0, :, pl.ds(q * LANES, LANES)] = turn_ref[pl.ds(q, 16, stride=8), :]


def stack(lags):
    vmem = pl.BlockSpec(memory_space=pltpu.VMEM)
    return pl.pallas_call(
        stack_kernel,
        out_shape=jax.ShapeDtypeStruct((1, 16, LAGS), jnp.float32),
        in_specs=[vmem],
        out_specs=vmem,
        scratch_shapes=[pltpu.VMEM((16 * 8, LANES), jnp.float32)],
        name="stack",
    )(lags)


def body(raw, pair_blocks):
    core = lax.axis_index("blk") % 2
    near = [[32 * (2 * t + h) + d for h in range(2) for d in range(32)] for t in range(4)]
    far = [
        [32 * (2 * t + h) + 2 * chip + c for t in range(4) for chip in range(16)]
        for h in range(2)
        for c in range(2)
    ]
    spectra = whiten(raw).reshape(64, 2 * 2 * SLOTS, LANES)
    spectra = lax.all_to_all(spectra, AXES, 0, 0, axis_index_groups=near, tiled=True)
    spectra = spectra.reshape(64, 2, 2 * SLOTS, LANES)
    order = pair_blocks.reshape(16, 2, 2)
    order = jnp.where(core == 0, order, order[:, ::-1]).transpose(2, 1, 0).reshape(2, 32)
    keep, send = correlate(order, spectra)
    got = lax.ppermute(send, "blk", [(i, i ^ 1) for i in range(32)])
    lags = jnp.where(core == 0, jnp.stack([keep, got]), jnp.stack([got, keep]))
    lags = lax.all_to_all(lags.reshape(64, 8, LANES), AXES, 0, 0, axis_index_groups=far, tiled=True)
    return stack(lags.reshape(4, 16, 8, LANES))


def solution(mesh):
    in_specs = (P("section", "blk", None), P())
    out_specs = P("blk", "section", None)
    return jax.shard_map(body, mesh=mesh, in_specs=in_specs, out_specs=out_specs, check_vma=False)
```

```python
import math

import jax
import jax.numpy as jnp
import ml_dtypes
import numpy as np
from jax import lax
from jax.experimental import pallas as pl
from jax.experimental.pallas import tpu as pltpu
from jax.sharding import PartitionSpec as P

NF = 8192
LAGS = 1024
LANES = 128
ROWS = 32
STEPS = 4
SLOTS = 32
TURN = 72
CHUNKS = 4
HALF = math.sqrt(0.5)
AXES = ("section", "blk")
RESIDUES = (
    [8, 16, 24]
    + [4 + 8 * r for r in range(4)]
    + [q + 8 * r for q in (1, 2, 3) for r in range(8)]
)


def bin_numbers():
    lane = np.arange(LANES)
    first = np.where(lane < 64, 64 * (lane + 1), 32 + 64 * (lane - 64))
    return np.stack([first] + [r + 64 * lane for r in RESIDUES])


def twiddles():
    lane = np.arange(LANES)
    turns = [lane / 128.0, lane / 256.0 + lane / 2.0] + [lane * r / NF for r in RESIDUES]
    angle = 2.0 * np.pi * np.stack(turns)
    return np.stack([np.cos(angle), np.sin(angle)]).astype(np.float32)


def last_transform():
    index = np.arange(LANES)
    angle = 2.0 * np.pi * (index[:, None] * index[None, :] % LANES) / LANES
    cosine, sine = np.cos(angle), np.sin(angle)
    full = np.block([[cosine, -sine], [sine, cosine]])
    high = full.astype(ml_dtypes.bfloat16)
    low = (full - high.astype(np.float64)).astype(ml_dtypes.bfloat16)
    return np.concatenate([high, high, low])


def lag_tables():
    bins = bin_numbers().reshape(-1)
    weight = np.where(bins == NF // 2, 0.5, 1.0)[:, None]
    angle = 2.0 * np.pi * (bins[:, None] * np.arange(LAGS // 2)[None, :] % NF) / NF
    cosine, sine = np.cos(angle), np.sin(angle)
    sine[:, 0] = np.sin(2.0 * np.pi * (bins * (LAGS // 2) % NF) / NF)
    tables = np.stack([cosine, sine]).astype(ml_dtypes.bfloat16).astype(np.float32) * weight
    return tables.astype(ml_dtypes.bfloat16).reshape(2 * CHUNKS, -1, LAGS // 2)


def far_cosines():
    bins = bin_numbers()[:, LANES - 1]
    return [float(c) for c in np.cos(2.0 * np.pi * (bins * 512 % NF) / NF).astype(ml_dtypes.bfloat16)]


def real8(x):
    s0, d0, s2, d2 = x[0] + x[4], x[0] - x[4], x[2] + x[6], x[2] - x[6]
    s1, d1, s3, d3 = x[1] + x[5], x[1] - x[5], x[3] + x[7], x[3] - x[7]
    even, odd = s0 + s2, s1 + s3
    u, v = (d1 - d3) * HALF, (d1 + d3) * HALF
    return [
        (even + odd, None),
        (d0 + u, -(d2 + v)),
        (s0 - s2, s3 - s1),
        (d0 - u, d2 - v),
        (even - odd, None),
    ]


def complex8(re, im):
    def add(i, j):
        return (i[0] + j[0], i[1] + j[1])

    def sub(i, j):
        return (i[0] - j[0], i[1] - j[1])

    def sub_i(i, j):
        return (i[0] + j[1], i[1] - j[0])

    def add_i(i, j):
        return (i[0] - j[1], i[1] + j[0])

    t = list(zip(re, im))
    a0, a1, a2, a3 = add(t[0], t[4]), sub(t[0], t[4]), add(t[2], t[6]), sub(t[2], t[6])
    a4, a5, a6, a7 = add(t[1], t[5]), sub(t[1], t[5]), add(t[3], t[7]), sub(t[3], t[7])
    b0, b2, b1, b3 = add(a0, a2), sub(a0, a2), sub_i(a1, a3), add_i(a1, a3)
    b4, b6, b5, b7 = add(a4, a6), sub(a4, a6), sub_i(a5, a7), add_i(a5, a7)
    c5 = ((b5[0] + b5[1]) * HALF, (b5[1] - b5[0]) * HALF)
    c7 = ((b7[1] - b7[0]) * HALF, (b7[0] + b7[1]) * -HALF)
    return [
        add(b0, b4), add(b1, c5), sub_i(b2, b6), add(b3, c7),
        sub(b0, b4), sub(b1, c5), add_i(b2, b6), sub(b3, c7),
    ]


def outer_transform(raw_ref, twist_ref, high_ref, low_ref, part_ref):
    f32, bf16 = jnp.float32, jnp.bfloat16

    def put(slot, re, im):
        cosine, sine = twist_ref[0, slot : slot + 1, :], twist_ref[1, slot : slot + 1, :]
        if im is None:
            zr, zi = re * cosine, re * -sine
        else:
            zr, zi = re * cosine + im * sine, im * cosine - re * sine
        rows = pl.ds(slot * ROWS, ROWS)
        for z, lanes in ((zr, pl.ds(0, LANES)), (zi, pl.ds(LANES, LANES))):
            high = z.astype(bf16)
            high_ref[rows, lanes] = high
            low_ref[rows, lanes] = (z - high.astype(f32)).astype(bf16)

    for b in range(8):
        x = [raw_ref[:, pl.ds((8 * a + b) * LANES, LANES)].astype(f32) for a in range(8)]
        y = real8(x)
        for q in range(5):
            part_ref[0, q, b] = y[q][0]
            if y[q][1] is not None:
                part_ref[1, q, b] = y[q][1]
    whole = real8([part_ref[0, 0, b] for b in range(8)])
    zero = whole[0][0] - jnp.mean(whole[0][0], axis=-1, keepdims=True)
    put(0, zero, None)
    put(1, whole[4][0], None)
    for r in (1, 2, 3):
        put(1 + r, *whole[r])
    slot = 5
    for q in (4, 1, 2, 3):
        re, im = [], []
        for b in range(8):
            cosine, sine = math.cos(2 * math.pi * b * q / 64), math.sin(2 * math.pi * b * q / 64)
            yr = part_ref[0, q, b]
            if q == 4:
                re.append(yr * cosine if b else yr)
                im.append(yr * -sine if b else jnp.zeros_like(yr))
            else:
                yi = part_ref[1, q, b]
                re.append(yr * cosine + yi * sine if b else yr)
                im.append(yi * cosine - yr * sine if b else yi)
        z = complex8(re, im)
        for r in range(4 if q == 4 else 8):
            put(slot, *z[r])
            slot += 1

def inner_transform(last_ref, high_ref, low_ref, spec_ref):
    high, low = high_ref[...], low_ref[...]
    left = jnp.concatenate([high, low, high], axis=1)
    spec_ref[...] = jnp.dot(left, last_ref[...], preferred_element_type=jnp.float32)


def level_rows(spec_ref, out_ref, turn_ref):
    bf16 = jnp.bfloat16
    lane = lax.broadcasted_iota(jnp.int32, (ROWS, LANES), 1)

    def get(slot):
        re = spec_ref[pl.ds((slot + 1) * ROWS, ROWS), pl.ds(0, LANES)]
        im = spec_ref[pl.ds((slot + 1) * ROWS, ROWS), pl.ds(LANES, LANES)]
        if slot == 0:
            re = jnp.where(lane < 64, spec_ref[pl.ds(0, ROWS), pl.ds(0, LANES)], re)
            im = jnp.where(lane < 64, spec_ref[pl.ds(0, ROWS), pl.ds(LANES, LANES)], im)
        return re, im

    total = None
    for slot in range(SLOTS):
        re, im = get(slot)
        power = re * re + im * im
        if slot == 0:
            power = jnp.where(lane == 63, power * 0.5, power)
        total = power if total is None else total + power
    level = jnp.sum(total, axis=-1, keepdims=True) * (2.0 / NF)
    floor = jnp.broadcast_to(0.1 * level + 1e-06, (ROWS, LANES))
    for slot in range(SLOTS):
        re, im = get(slot)
        scale = lax.rsqrt(re * re + im * im + floor)
        turn_ref[pl.ds(slot, ROWS, stride=TURN), :] = re * scale
        turn_ref[pl.ds(slot + SLOTS, ROWS, stride=TURN), :] = im * scale
    for r in range(ROWS):
        out_ref[r // 16, r % 16] = turn_ref[pl.ds(r * TURN, 2 * SLOTS), :].astype(bf16)


def whiten_kernel(
    raw_hbm, twist_hbm, last_hbm, out_hbm, raw_ref, twist_ref, last_ref, out_ref, in_sem, table_sem, out_sem, *work
):
    def fetch(g):
        return pltpu.make_async_copy(raw_hbm.at[0, pl.ds(g * ROWS, ROWS)], raw_ref.at[g], in_sem.at[g])

    def leave(g):
        return pltpu.make_async_copy(out_ref.at[g], out_hbm.at[:, :, g // 2, g % 2], out_sem.at[g])

    twist = pltpu.make_async_copy(twist_hbm, twist_ref, table_sem.at[0])
    last = pltpu.make_async_copy(last_hbm, last_ref, table_sem.at[1])
    fetch(0).start()
    twist.start()
    last.start()
    for g in range(1, STEPS):
        fetch(g).start()
    part, high, low, spec, turn = work

    def outer(g):
        outer_transform(raw_ref.at[g], twist_ref, high, low, part)

    twist.wait()
    fetch(0).wait()
    outer(0)
    last.wait()

    def step(g, carry):
        fetch(g + 1).wait()
        inner_transform(last_ref, high, low, spec)
        outer(g + 1)
        level_rows(spec, out_ref.at[g], turn)

        leave(g).start()
        return carry

    lax.fori_loop(0, STEPS - 1, step, 0)
    inner_transform(last_ref, high, low, spec)
    level_rows(spec, out_ref.at[STEPS - 1], turn)
    leave(STEPS - 1).start()
    for g in range(STEPS):
        leave(g).wait()


def whiten(raw):
    far = pl.BlockSpec(memory_space=pltpu.HBM)
    return pl.pallas_call(
        whiten_kernel,
        out_shape=jax.ShapeDtypeStruct((2, 16, 2, 2, 2 * SLOTS, LANES), jnp.bfloat16),
        in_specs=[far] * 3,
        out_specs=far,
        scratch_shapes=[
            pltpu.VMEM((STEPS, ROWS, NF), jnp.bfloat16),
            pltpu.VMEM((2, SLOTS + 1, LANES), jnp.float32),
            pltpu.VMEM((6 * LANES, 2 * LANES), jnp.bfloat16),
            pltpu.VMEM((STEPS, 2, 16, 2 * SLOTS, LANES), jnp.bfloat16),
            pltpu.SemaphoreType.DMA((STEPS,)),
            pltpu.SemaphoreType.DMA((2,)),
            pltpu.SemaphoreType.DMA((STEPS,)),
        ]
        + [
            pltpu.VMEM((2, 5, 8, ROWS, LANES), jnp.float32),
            pltpu.VMEM(((SLOTS + 1) * ROWS, 2 * LANES), jnp.bfloat16),
            pltpu.VMEM(((SLOTS + 1) * ROWS, 2 * LANES), jnp.bfloat16),
            pltpu.VMEM(((SLOTS + 1) * ROWS, 2 * LANES), jnp.float32),
            pltpu.VMEM((ROWS * TURN, LANES), jnp.float32),
        ],
        compiler_params=pltpu.CompilerParams(vmem_limit_bytes=60 * 2**20),
        name="whiten",
    )(raw, jnp.asarray(twiddles()), jnp.asarray(last_transform()))


def lag_kernel(
    pairs_ref, spec_ref, table_hbm, keep_ref, send_ref, cross_ref, left_ref, table_ref, turn_ref, table_sem
):
    f32, bf16 = jnp.float32, jnp.bfloat16
    depth = table_ref.shape[1]

    def fetch(c):
        return pltpu.make_async_copy(table_hbm.at[c], table_ref.at[c], table_sem.at[c])

    for c in range(2 * CHUNKS):
        fetch(c).start()

    def one(i, carry):
        first, second = pairs_ref[0, i], pairs_ref[1, i]
        for h in range(2):
            for j in range(2):
                a = spec_ref[h * 32 + first, j].astype(f32)
                b = spec_ref[h * 32 + second, j].astype(f32)
                ar, ai, br, bi = a[:SLOTS], a[SLOTS:], b[:SLOTS], b[SLOTS:]
                row = pl.multiple_of(((h * 2 + j) * 32 + i) * TURN, 8)
                cross_ref[pl.ds(row, SLOTS), :] = ar * br + ai * bi
                cross_ref[pl.ds(row + SLOTS, SLOTS), :] = ai * br - ar * bi
        return carry

    lax.fori_loop(0, 32, one, 0)
    far = None
    for slot, cosine in enumerate(far_cosines()):
        cross = cross_ref[pl.ds(slot, 128, stride=TURN), :].astype(bf16)
        left_ref[:, pl.ds(slot * LANES, LANES)] = cross
        term = cross.astype(f32)
        if slot == 0:
            lane = lax.broadcasted_iota(jnp.int32, (128, LANES), 1)
            far = jnp.where(lane == 63, 0.5, cosine) * term
        elif cosine != 0.0:
            far = far + term * cosine
    far = jnp.sum(far[:64] + far[64:], axis=-1, keepdims=True)
    for slot in range(SLOTS, 2 * SLOTS):
        left_ref[:, pl.ds(slot * LANES, LANES)] = cross_ref[pl.ds(slot, 128, stride=TURN), :].astype(bf16)

    halves = []
    for part in range(2):
        total = None
        for c in range(part * CHUNKS, (part + 1) * CHUNKS):
            fetch(c).wait()
            term = jnp.dot(left_ref[:, pl.ds(c * depth, depth)], table_ref[c], preferred_element_type=f32)
            total = term if total is None else total + term
        halves.append(total[:64] + total[64:])
    even, odd = halves
    lane = lax.broadcasted_iota(jnp.int32, (64, LANES), 1)
    for q in range(4):
        e, o = even[:, q * LANES : (q + 1) * LANES], odd[:, q * LANES : (q + 1) * LANES]
        minus, plus = e + o, e - o
        if q == 0:
            minus, plus = jnp.where(lane == 0, far + o, minus), jnp.where(lane == 0, e, plus)
        turn_ref[pl.ds(q, 64, stride=8), :] = minus * (2.0 * NF**-0.5)
        turn_ref[pl.ds(q + 4, 64, stride=8), :] = plus * (2.0 * NF**-0.5)
    turned = turn_ref[...].reshape(2, 2, 16, 8, LANES)
    keep_ref[...] = turned[:, 0].astype(bf16)
    send_ref[...] = turned[:, 1].astype(bf16)


def correlate(pairs, spectra):
    half = jax.ShapeDtypeStruct((2, 16, 8, LANES), jnp.bfloat16)
    vmem = pl.BlockSpec(memory_space=pltpu.VMEM)
    tables = pltpu.with_memory_space_constraint(jnp.asarray(lag_tables()), pltpu.HBM)
    return pl.pallas_call(
        lag_kernel,
        out_shape=(half, half),
        in_specs=[pl.BlockSpec(memory_space=pltpu.SMEM), vmem, pl.BlockSpec(memory_space=pltpu.HBM)],
        out_specs=(vmem, vmem),
        scratch_shapes=[
            pltpu.VMEM((128 * TURN, LANES), jnp.float32),
            pltpu.VMEM((128, NF), jnp.bfloat16),
            pltpu.VMEM(tables.shape, jnp.bfloat16),
            pltpu.VMEM((64 * 8, LANES), jnp.float32),
            pltpu.SemaphoreType.DMA((2 * CHUNKS,)),
        ],
        compiler_params=pltpu.CompilerParams(vmem_limit_bytes=24 * 2**20),
        name="correlate",
    )(pairs, spectra, tables)


def stack_kernel(lags_ref, out_ref, turn_ref):
    total = lags_ref[0].astype(jnp.float32)
    for t in range(1, 4):
        total = total + lags_ref[t].astype(jnp.float32)
    turn_ref[...] = total.reshape(16 * 8, LANES)
    runs = [turn_ref[pl.ds(q, 16, stride=8), :] for q in range(8)]
    lane = lax.broadcasted_iota(jnp.int32, (16, LANES), 1)
    back = (LANES - lane) % LANES
    runs[:4] = [jnp.take_along_axis(run, back, axis=1, mode="promise_in_bounds") for run in runs[:4]]
    for q in range(4):
        out_ref[0, :, pl.ds(q * LANES, LANES)] = jnp.where(lane == 0, runs[(4 - q) % 4], runs[3 - q])
    for q in range(4, 8):
        out_ref[0, :, pl.ds(q * LANES, LANES)] = runs[q]


def stack(lags):
    vmem = pl.BlockSpec(memory_space=pltpu.VMEM)
    return pl.pallas_call(
        stack_kernel,
        out_shape=jax.ShapeDtypeStruct((1, 16, LAGS), jnp.float32),
        in_specs=[vmem],
        out_specs=vmem,
        scratch_shapes=[pltpu.VMEM((16 * 8, LANES), jnp.float32)],
        name="stack",
    )(lags)


def body(raw, pair_blocks):
    core = lax.axis_index("blk") % 2
    near = [[32 * (2 * t + h) + d for h in range(2) for d in range(32)] for t in range(4)]
    far = [
        [32 * (2 * t + h) + 2 * chip + c for t in range(4) for chip in range(16)]
        for h in range(2)
        for c in range(2)
    ]
    spectra = whiten(raw).reshape(64, 2 * 2 * SLOTS, LANES)
    spectra = lax.all_to_all(spectra, AXES, 0, 0, axis_index_groups=near, tiled=True)
    spectra = spectra.reshape(64, 2, 2 * SLOTS, LANES)
    order = pair_blocks.reshape(16, 2, 2)
    order = jnp.where(core == 0, order, order[:, ::-1]).transpose(2, 1, 0).reshape(2, 32)
    keep, send = correlate(order, spectra)
    got = lax.ppermute(send, "blk", [(i, i ^ 1) for i in range(32)])
    lags = jnp.where(core == 0, jnp.stack([keep, got]), jnp.stack([got, keep]))
    lags = lax.all_to_all(lags.reshape(64, 8, LANES), AXES, 0, 0, axis_index_groups=far, tiled=True)
    return stack(lags.reshape(4, 16, 8, LANES))


def solution(mesh):
    in_specs = (P("section", "blk", None), P())
    out_specs = P("blk", "section", None)
    return jax.shard_map(body, mesh=mesh, in_specs=in_specs, out_specs=out_specs, check_vma=False)
```

```python
import math

import jax
import jax.numpy as jnp
import ml_dtypes
import numpy as np
from jax import lax
from jax.experimental import pallas as pl
from jax.experimental.pallas import tpu as pltpu
from jax.sharding import PartitionSpec as P

NF = 8192
LAGS = 1024
LANES = 128
ROWS = 32
STEPS = 4
SLOTS = 32
TURN = 72
CHUNKS = 4
HALF = math.sqrt(0.5)
AXES = ("section", "blk")
RESIDUES = (
    [8, 16, 24]
    + [4 + 8 * r for r in range(4)]
    + [q + 8 * r for q in (1, 2, 3) for r in range(8)]
)


def bin_numbers():
    lane = np.arange(LANES)
    first = np.where(lane % 64 < 32, 64 * lane, 32 + 64 * (lane - 32))
    first[0] = 2048
    return np.stack([first] + [r + 64 * lane for r in RESIDUES])


def twiddles():
    lane = np.arange(LANES)
    turns = [lane / 256.0 - lane / 4.0] + [lane * r / NF for r in RESIDUES]
    angle = 2.0 * np.pi * np.stack(turns)
    return np.stack([np.cos(angle), np.sin(angle)]).astype(np.float32)


def last_transform():
    index = np.arange(LANES)
    angle = 2.0 * np.pi * (index[:, None] * index[None, :] % LANES) / LANES
    cosine, sine = np.cos(angle), np.sin(angle)
    full = np.block([[cosine, -sine], [sine, cosine]])
    return full.astype(np.float32)


def folded_bins():
    bins = bin_numbers()
    return np.concatenate([bins[:16, :64], bins[16:, :64]], axis=1)


def lag_tables():
    bins = folded_bins().reshape(-1)[:, None]
    even, odd = 2 * np.arange(256)[None, :], 2 * np.arange(256)[None, :] + 1
    sign = np.where(np.arange(LANES) < 64, 1.0, -1.0)[None, :, None]
    tables = []
    for function, first in ((np.cos, 0), (np.sin, 512)):
        near = function(2.0 * np.pi * (bins * np.where(even == 0, first, even) % NF) / NF)
        far = function(2.0 * np.pi * (bins * odd % NF) / NF).reshape(16, LANES, 256) * sign
        tables.append(np.concatenate([near, far.reshape(-1, 256)], axis=1))
    return np.stack(tables).astype(ml_dtypes.bfloat16).reshape(2 * CHUNKS, -1, 512)


def far_cosines():
    bins = folded_bins()[:, [1, LANES - 1]]
    cosines = np.cos(2.0 * np.pi * (bins * 512 % NF) / NF).astype(ml_dtypes.bfloat16)
    return [(float(low), float(high)) for low, high in cosines]


def real8(x):
    s0, d0, s2, d2 = x[0] + x[4], x[0] - x[4], x[2] + x[6], x[2] - x[6]
    s1, d1, s3, d3 = x[1] + x[5], x[1] - x[5], x[3] + x[7], x[3] - x[7]
    even, odd = s0 + s2, s1 + s3
    u, v = (d1 - d3) * HALF, (d1 + d3) * HALF
    return [
        (even + odd, None),
        (d0 + u, -(d2 + v)),
        (s0 - s2, s3 - s1),
        (d0 - u, d2 - v),
        (even - odd, None),
    ]


def complex8(re, im):
    def add(i, j):
        return (i[0] + j[0], i[1] + j[1])

    def sub(i, j):
        return (i[0] - j[0], i[1] - j[1])

    def sub_i(i, j):
        return (i[0] + j[1], i[1] - j[0])

    def add_i(i, j):
        return (i[0] - j[1], i[1] + j[0])

    t = list(zip(re, im))
    a0, a1, a2, a3 = add(t[0], t[4]), sub(t[0], t[4]), add(t[2], t[6]), sub(t[2], t[6])
    a4, a5, a6, a7 = add(t[1], t[5]), sub(t[1], t[5]), add(t[3], t[7]), sub(t[3], t[7])
    b0, b2, b1, b3 = add(a0, a2), sub(a0, a2), sub_i(a1, a3), add_i(a1, a3)
    b4, b6, b5, b7 = add(a4, a6), sub(a4, a6), sub_i(a5, a7), add_i(a5, a7)
    c5 = ((b5[0] + b5[1]) * HALF, (b5[1] - b5[0]) * HALF)
    c7 = ((b7[1] - b7[0]) * HALF, (b7[0] + b7[1]) * -HALF)
    return [
        add(b0, b4), add(b1, c5), sub_i(b2, b6), add(b3, c7),
        sub(b0, b4), sub(b1, c5), add_i(b2, b6), sub(b3, c7),
    ]


def outer_transform(raw_ref, twist_ref, turned_ref, part_ref):
    f32 = jnp.float32

    def put(slot, re, im):
        rows = pl.ds(slot * ROWS, ROWS)
        turned_ref[rows, pl.ds(0, LANES)] = re
        turned_ref[rows, pl.ds(LANES, LANES)] = im

    def turn(slot, re, im):
        cosine, sine = twist_ref[0, slot - 1 : slot, :], twist_ref[1, slot - 1 : slot, :]
        if im is None:
            put(slot, re * cosine, re * -sine)
        else:
            put(slot, re * cosine + im * sine, im * cosine - re * sine)

    for b in range(8):
        x = [raw_ref[:, pl.ds((8 * a + b) * LANES, LANES)].astype(f32) for a in range(8)]
        y = real8(x)
        for q in range(5):
            part_ref[0, q, b] = y[q][0]
            if y[q][1] is not None:
                part_ref[1, q, b] = y[q][1]
    whole = real8([part_ref[0, 0, b] for b in range(8)])
    zero = whole[0][0]
    put(0, zero - jnp.mean(zero, axis=-1, keepdims=True), jnp.zeros_like(zero))
    turn(1, whole[4][0], None)
    for r in (1, 2, 3):
        turn(1 + r, *whole[r])
    slot = 5
    for q in (4, 1, 2, 3):
        re, im = [], []
        for b in range(8):
            cosine, sine = math.cos(2 * math.pi * b * q / 64), math.sin(2 * math.pi * b * q / 64)
            yr = part_ref[0, q, b]
            if q == 4:
                re.append(yr * cosine if b else yr)
                im.append(yr * -sine if b else jnp.zeros_like(yr))
            else:
                yi = part_ref[1, q, b]
                re.append(yr * cosine + yi * sine if b else yr)
                im.append(yi * cosine - yr * sine if b else yi)
        z = complex8(re, im)
        for r in range(4 if q == 4 else 8):
            turn(slot, *z[r])
            slot += 1

def inner_transform(last_ref, turned_ref, spec_ref):
    spec_ref[...] = jnp.dot(
        turned_ref[...], last_ref[...], preferred_element_type=jnp.float32, precision=lax.Precision.HIGH
    )


def level_rows(spec_ref, out_ref, turn_ref):
    bf16 = jnp.bfloat16
    lane = lax.broadcasted_iota(jnp.int32, (ROWS, LANES), 1)

    for lanes in (pl.ds(0, LANES), pl.ds(LANES, LANES)):
        whole, moved = spec_ref[pl.ds(0, ROWS), lanes], spec_ref[pl.ds(ROWS, ROWS), lanes]
        whole = jnp.where(lane == 0, pltpu.roll(whole, 96, 1), whole)
        spec_ref[pl.ds(ROWS, ROWS), lanes] = jnp.where(lane % 64 < 32, whole, moved)

    def get(slot):
        rows = pl.ds((slot + 1) * ROWS, ROWS)
        return spec_ref[rows, pl.ds(0, LANES)], spec_ref[rows, pl.ds(LANES, LANES)]

    total = None
    for slot in range(SLOTS):
        re, im = get(slot)
        power = re * re + im * im
        if slot == 0:
            power = jnp.where(lane == 64, power * 0.5, power)
        total = power if total is None else total + power
    level = jnp.sum(total, axis=-1, keepdims=True) * (2.0 / NF)
    floor = jnp.broadcast_to(0.1 * level + 1e-06, (ROWS, LANES))
    for slot in range(SLOTS):
        re, im = get(slot)
        scale = lax.rsqrt(re * re + im * im + floor)
        turn_ref[pl.ds(slot, ROWS, stride=TURN), :] = re * scale
        turn_ref[pl.ds(slot + SLOTS, ROWS, stride=TURN), :] = im * scale
    for r in range(ROWS):
        out_ref[r // 16, r % 16] = turn_ref[pl.ds(r * TURN, 2 * SLOTS), :].astype(bf16)


def whiten_kernel(
    raw_hbm, twist_hbm, last_hbm, out_hbm, raw_ref, twist_ref, last_ref, out_ref, in_sem, table_sem, out_sem, *work
):
    def fetch(g):
        return pltpu.make_async_copy(raw_hbm.at[0, pl.ds(g * ROWS, ROWS)], raw_ref.at[g], in_sem.at[g])

    def leave(g):
        return pltpu.make_async_copy(out_ref.at[g], out_hbm.at[:, :, g // 2, g % 2], out_sem.at[g])

    twist = pltpu.make_async_copy(twist_hbm, twist_ref, table_sem.at[0])
    last = pltpu.make_async_copy(last_hbm, last_ref, table_sem.at[1])
    fetch(0).start()
    twist.start()
    last.start()
    for g in range(1, STEPS):
        fetch(g).start()
    part, turned, spec, turn = work

    def outer(g):
        outer_transform(raw_ref.at[g], twist_ref, turned, part)

    twist.wait()
    fetch(0).wait()
    outer(0)
    last.wait()

    def step(g, carry):
        fetch(g + 1).wait()
        inner_transform(last_ref, turned, spec)
        outer(g + 1)
        level_rows(spec, out_ref.at[g], turn)

        leave(g).start()
        return carry

    lax.fori_loop(0, STEPS - 1, step, 0)
    inner_transform(last_ref, turned, spec)
    level_rows(spec, out_ref.at[STEPS - 1], turn)
    leave(STEPS - 1).start()
    for g in range(STEPS):
        leave(g).wait()


def whiten(raw):
    far = pl.BlockSpec(memory_space=pltpu.HBM)
    return pl.pallas_call(
        whiten_kernel,
        out_shape=jax.ShapeDtypeStruct((2, 16, 2, 2, 2 * SLOTS, LANES), jnp.bfloat16),
        in_specs=[far] * 3,
        out_specs=far,
        scratch_shapes=[
            pltpu.VMEM((STEPS, ROWS, NF), jnp.bfloat16),
            pltpu.VMEM((2, SLOTS, LANES), jnp.float32),
            pltpu.VMEM((2 * LANES, 2 * LANES), jnp.float32),
            pltpu.VMEM((STEPS, 2, 16, 2 * SLOTS, LANES), jnp.bfloat16),
            pltpu.SemaphoreType.DMA((STEPS,)),
            pltpu.SemaphoreType.DMA((2,)),
            pltpu.SemaphoreType.DMA((STEPS,)),
        ]
        + [
            pltpu.VMEM((2, 5, 8, ROWS, LANES), jnp.float32),
            pltpu.VMEM(((SLOTS + 1) * ROWS, 2 * LANES), jnp.float32),
            pltpu.VMEM(((SLOTS + 1) * ROWS, 2 * LANES), jnp.float32),
            pltpu.VMEM((ROWS * TURN, LANES), jnp.float32),
        ],
        compiler_params=pltpu.CompilerParams(vmem_limit_bytes=60 * 2**20),
        name="whiten",
    )(raw, jnp.asarray(twiddles()), jnp.asarray(last_transform()))


def lag_kernel(
    pairs_ref, spec_ref, table_hbm, keep_ref, send_ref, cross_ref, left_ref, table_ref, turn_ref, table_sem
):
    f32, bf16 = jnp.float32, jnp.bfloat16
    depth = table_ref.shape[1]
    half = SLOTS // 2

    def fetch(c):
        return pltpu.make_async_copy(table_hbm.at[c], table_ref.at[c], table_sem.at[c])

    for c in range(2 * CHUNKS):
        fetch(c).start()

    lower = lax.broadcasted_iota(jnp.int32, (half, LANES), 1) < 64

    def one(i, carry):
        pair = pairs_ref[pl.ds(i, 1), :]
        first, second = pair[0, 0], pair[0, 1]
        for h in range(2):
            for j in range(2):
                a = spec_ref[h * 32 + first, j].astype(f32)
                b = spec_ref[h * 32 + second, j].astype(f32)
                ar, ai, br, bi = a[:SLOTS], a[SLOTS:], b[:SLOTS], b[SLOTS:]
                row = pl.multiple_of(((h * 2 + j) * 32 + i) * TURN, 8)
                for part, cross in ((0, ar * br + ai * bi), (1, ai * br - ar * bi)):
                    near = jnp.where(lower, cross[:half], cross[half:])
                    away = pltpu.roll(jnp.where(lower, cross[half:], cross[:half]), 64, 1)
                    cross_ref[pl.ds(row + part * half, half), :] = near
                    cross_ref[pl.ds(row + (2 + part) * half, half), :] = away
        return carry

    lax.fori_loop(0, 32, one, 0, unroll=8)
    lane = lax.broadcasted_iota(jnp.int32, (128, LANES), 1)
    cosines = far_cosines()
    far, middle = None, None
    for side in range(2):
        for slot in range(SLOTS):
            cross = cross_ref[pl.ds(side * SLOTS + slot, 128, stride=TURN), :].astype(bf16)
            term = cross.astype(f32) if slot < half else None
            if side == 1 and slot % half == 0:
                if slot == 0:
                    middle = 0.5 * term[:, :1]
                    term = jnp.where(lane == 0, 0.0, term)
                cross = jnp.where(lane == 0, jnp.zeros_like(cross), cross)
            left_ref[pl.ds(side * 128, 128), pl.ds(slot * LANES, LANES)] = cross
            if slot < half:
                term = term * jnp.where(lane < 64, *cosines[slot])
                far = term if far is None else far + term
    far = jnp.sum(far, axis=-1, keepdims=True) + middle
    far, middle = far[:64] + far[64:], middle[:64] + middle[64:]

    for c in range(2 * CHUNKS):
        fetch(c).wait()
    sums = []
    for part in range(2):
        total = None
        for c in range(part * CHUNKS, (part + 1) * CHUNKS):
            left = left_ref[:, pl.ds(c * depth, depth)]
            term = jnp.dot(left, table_ref[c], preferred_element_type=f32)
            total = term if total is None else total + term
        near, away = total[:64] + total[64:128], total[128:192] + total[192:]
        sums.append((near[:, :256] + away[:, :256], near[:, 256:] - away[:, 256:]))
    (even_cosine, odd_cosine), (even_sine, odd_sine) = sums
    even_cosine, odd_cosine = even_cosine + middle, odd_cosine - middle
    lane = lax.broadcasted_iota(jnp.int32, (64, LANES), 1)
    for q in range(2):
        run = slice(q * LANES, (q + 1) * LANES)
        c, s = even_cosine[:, run], even_sine[:, run]
        minus, plus = c + s, c - s
        if q == 0:
            minus, plus = jnp.where(lane == 0, far + s, minus), jnp.where(lane == 0, c, plus)
        c, s = odd_cosine[:, run], odd_sine[:, run]
        for place, lags in ((q, minus), (q + 2, c + s), (q + 4, plus), (q + 6, c - s)):
            turn_ref[pl.ds(place, 64, stride=8), :] = lags * (2.0 * NF**-0.5)
    turned = turn_ref[...].reshape(2, 2, 16, 8, LANES)
    keep_ref[...] = turned[:, 0].astype(bf16)
    send_ref[...] = turned[:, 1].astype(bf16)


def correlate(pairs, spectra):
    half = jax.ShapeDtypeStruct((2, 16, 8, LANES), jnp.bfloat16)
    vmem = pl.BlockSpec(memory_space=pltpu.VMEM)
    tables = pltpu.with_memory_space_constraint(jnp.asarray(lag_tables()), pltpu.HBM)
    return pl.pallas_call(
        lag_kernel,
        out_shape=(half, half),
        in_specs=[vmem, vmem, pl.BlockSpec(memory_space=pltpu.HBM)],
        out_specs=(vmem, vmem),
        scratch_shapes=[
            pltpu.VMEM((128 * TURN, LANES), jnp.float32),
            pltpu.VMEM((256, NF // 2), jnp.bfloat16),
            pltpu.VMEM(tables.shape, jnp.bfloat16),
            pltpu.VMEM((64 * 8, LANES), jnp.float32),
            pltpu.SemaphoreType.DMA((2 * CHUNKS,)),
        ],
        compiler_params=pltpu.CompilerParams(vmem_limit_bytes=24 * 2**20),
        name="correlate",
    )(pairs, spectra, tables)


def stack_kernel(lags_ref, out_ref, turn_ref):
    total = lags_ref[0].astype(jnp.float32)
    for t in range(1, 4):
        total = total + lags_ref[t].astype(jnp.float32)
    turn_ref[...] = total.reshape(16 * 8, LANES)
    runs = [turn_ref[pl.ds(q, 16, stride=8), :] for q in range(8)]
    lane = lax.broadcasted_iota(jnp.int32, (16, LANES), 1)

    def pick(run, index):
        return jnp.take_along_axis(run, index, axis=1, mode="promise_in_bounds")

    for q in range(4):
        index = 64 * (q % 2) + lane // 2
        even, odd = pick(runs[4 + q // 2], index), pick(runs[6 + q // 2], index)
        out_ref[0, :, pl.ds((4 + q) * LANES, LANES)] = jnp.where(lane % 2 == 0, even, odd)
    for q in range(4):
        b, after = 3 - q, (4 - q) % 4
        even = pick(runs[b // 2], 64 * (b % 2) + (64 - lane // 2) % 64)
        first = pick(runs[after // 2], jnp.full_like(lane, 64 * (after % 2)))
        odd = pick(runs[2 + b // 2], 64 * (b % 2) + 63 - lane // 2)
        even = jnp.where(lane == 0, first, even)
        out_ref[0, :, pl.ds(q * LANES, LANES)] = jnp.where(lane % 2 == 0, even, odd)


def stack(lags):
    vmem = pl.BlockSpec(memory_space=pltpu.VMEM)
    return pl.pallas_call(
        stack_kernel,
        out_shape=jax.ShapeDtypeStruct((1, 16, LAGS), jnp.float32),
        in_specs=[vmem],
        out_specs=vmem,
        scratch_shapes=[pltpu.VMEM((16 * 8, LANES), jnp.float32)],
        name="stack",
    )(lags)


def body(raw, pair_blocks):
    core = lax.axis_index("blk") % 2
    near = [[32 * (2 * t + h) + d for h in range(2) for d in range(32)] for t in range(4)]
    far = [
        [32 * (2 * t + h) + 2 * chip + c for t in range(4) for chip in range(16)]
        for h in range(2)
        for c in range(2)
    ]
    spectra = whiten(raw).reshape(64, 2 * 2 * SLOTS, LANES)
    spectra = lax.all_to_all(spectra, AXES, 0, 0, axis_index_groups=near, tiled=True)
    spectra = spectra.reshape(64, 2, 2 * SLOTS, LANES)
    order = pair_blocks.reshape(16, 2, 2)
    order = jnp.where(core == 0, order, order[:, ::-1]).transpose(1, 0, 2).reshape(32, 2)
    order = jnp.pad(order, ((0, 0), (0, LANES - 2)))
    keep, send = correlate(order, spectra)
    got = lax.ppermute(send, "blk", [(i, i ^ 1) for i in range(32)])
    lags = jnp.where(core == 0, jnp.stack([keep, got]), jnp.stack([got, keep]))
    lags = lax.all_to_all(lags.reshape(64, 8, LANES), AXES, 0, 0, axis_index_groups=far, tiled=True)
    return stack(pltpu.with_memory_space_constraint(lags.reshape(4, 16, 8, LANES), pltpu.VMEM))


def solution(mesh):
    in_specs = (P("section", "blk", None), P())
    out_specs = P("blk", "section", None)
    return jax.shard_map(body, mesh=mesh, in_specs=in_specs, out_specs=out_specs, check_vma=False)
```

```python
import math

import jax
import jax.numpy as jnp
import ml_dtypes
import numpy as np
from jax import lax
from jax.experimental import pallas as pl
from jax.experimental.pallas import tpu as pltpu
from jax.sharding import PartitionSpec as P

NF = 8192
LAGS = 1024
LANES = 128
ROWS = 64
STEPS = 2
PART = 32
SLOTS = 32
TURN = 72
CHUNKS = 4
HALF = math.sqrt(0.5)
AXES = ("section", "blk")
RESIDUES = (
    [8, 16, 24]
    + [4 + 8 * r for r in range(4)]
    + [q + 8 * r for q in (1, 2, 3) for r in range(8)]
)


def bin_numbers():
    lane = np.arange(LANES)
    first = np.where(lane % 64 < 32, 64 * lane, 32 + 64 * (lane - 32))
    first[0] = 2048
    return np.stack([first] + [r + 64 * lane for r in RESIDUES])


def twiddles():
    lane = np.arange(LANES)
    turns = [lane / 256.0 - lane / 4.0] + [lane * r / NF for r in RESIDUES]
    angle = 2.0 * np.pi * np.stack(turns)
    return np.stack([np.cos(angle), np.sin(angle)]).astype(np.float32)


def last_transform():
    index = np.arange(LANES)
    angle = 2.0 * np.pi * (index[:, None] * index[None, :] % LANES) / LANES
    cosine, sine = np.cos(angle), np.sin(angle)
    full = np.block([[cosine, -sine], [sine, cosine]])
    high = full.astype(ml_dtypes.bfloat16)
    low = (full - high.astype(np.float64)).astype(ml_dtypes.bfloat16)
    return np.concatenate([high, high, low])


def folded_bins():
    bins = bin_numbers()
    return np.concatenate([bins[:16, :64], bins[16:, :64]], axis=1)


def folded_bins():
    bins = bin_numbers()
    return np.concatenate([bins[:16, :64], bins[16:, :64]], axis=1)


def lag_tables():
    bins = folded_bins().reshape(-1)[:, None]
    even, odd = 2 * np.arange(256)[None, :], 2 * np.arange(256)[None, :] + 1
    sign = np.where(np.arange(LANES) < 64, 1.0, -1.0)[None, :, None]
    tables = []
    for function, first in ((np.cos, 0), (np.sin, 512)):
        near = function(2.0 * np.pi * (bins * np.where(even == 0, first, even) % NF) / NF)
        far = function(2.0 * np.pi * (bins * odd % NF) / NF).reshape(16, LANES, 256) * sign
        tables.append(np.concatenate([near, far.reshape(-1, 256)], axis=1))
    return np.stack(tables).astype(ml_dtypes.bfloat16).reshape(2 * CHUNKS, -1, 512)


def far_cosines():
    bins = folded_bins()[:, [1, LANES - 1]]
    cosines = np.cos(2.0 * np.pi * (bins * 512 % NF) / NF).astype(ml_dtypes.bfloat16)
    return [(float(low), float(high)) for low, high in cosines]


def real8(x):
    s0, d0, s2, d2 = x[0] + x[4], x[0] - x[4], x[2] + x[6], x[2] - x[6]
    s1, d1, s3, d3 = x[1] + x[5], x[1] - x[5], x[3] + x[7], x[3] - x[7]
    even, odd = s0 + s2, s1 + s3
    u, v = (d1 - d3) * HALF, (d1 + d3) * HALF
    return [
        (even + odd, None),
        (d0 + u, -(d2 + v)),
        (s0 - s2, s3 - s1),
        (d0 - u, d2 - v),
        (even - odd, None),
    ]


def complex8(re, im):
    def add(i, j):
        return (i[0] + j[0], i[1] + j[1])

    def sub(i, j):
        return (i[0] - j[0], i[1] - j[1])

    def sub_i(i, j):
        return (i[0] + j[1], i[1] - j[0])

    def add_i(i, j):
        return (i[0] - j[1], i[1] + j[0])

    t = list(zip(re, im))
    a0, a1, a2, a3 = add(t[0], t[4]), sub(t[0], t[4]), add(t[2], t[6]), sub(t[2], t[6])
    a4, a5, a6, a7 = add(t[1], t[5]), sub(t[1], t[5]), add(t[3], t[7]), sub(t[3], t[7])
    b0, b2, b1, b3 = add(a0, a2), sub(a0, a2), sub_i(a1, a3), add_i(a1, a3)
    b4, b6, b5, b7 = add(a4, a6), sub(a4, a6), sub_i(a5, a7), add_i(a5, a7)
    c5 = ((b5[0] + b5[1]) * HALF, (b5[1] - b5[0]) * HALF)
    c7 = ((b7[1] - b7[0]) * HALF, (b7[0] + b7[1]) * -HALF)
    return [
        add(b0, b4), add(b1, c5), sub_i(b2, b6), add(b3, c7),
        sub(b0, b4), sub(b1, c5), add_i(b2, b6), sub(b3, c7),
    ]


def outer_transform(raw_ref, twist_ref, turned_ref, part_ref):
    f32 = jnp.float32
    for first in range(0, ROWS, 32):
        rows = pl.ds(first, 32)
        for b in range(8):
            x = [raw_ref[rows, pl.ds((8 * a + b) * LANES, LANES)].astype(f32) for a in range(8)]
            y = real8(x)
            for q in range(5):
                part_ref[0, q, b, rows] = y[q][0]
                if y[q][1] is not None:
                    part_ref[1, q, b, rows] = y[q][1]
    for first in range(0, ROWS, 8):
        second_transform(first, 8, twist_ref, turned_ref, part_ref)


def second_transform(first, count, twist_ref, turned_ref, part_ref):
    def put(slot, re, im):
        rows = pl.ds(slot * ROWS + first, count)
        turned_ref[rows, pl.ds(0, LANES)] = re
        turned_ref[rows, pl.ds(LANES, LANES)] = im

    def turn(slot, re, im):
        cosine, sine = twist_ref[0, slot - 1 : slot, :], twist_ref[1, slot - 1 : slot, :]
        if im is None:
            put(slot, re * cosine, re * -sine)
        else:
            put(slot, re * cosine + im * sine, im * cosine - re * sine)

    def part(side, q, b):
        return part_ref[side, q, b, pl.ds(first, count)]

    whole = real8([part(0, 0, b) for b in range(8)])
    zero = whole[0][0]
    put(0, zero - jnp.mean(zero, axis=-1, keepdims=True), jnp.zeros_like(zero))
    turn(1, whole[4][0], None)
    for r in (1, 2, 3):
        turn(1 + r, *whole[r])
    slot = 5
    for q in (4, 1, 2, 3):
        re, im = [], []
        for b in range(8):
            cosine, sine = math.cos(2 * math.pi * b * q / 64), math.sin(2 * math.pi * b * q / 64)
            yr = part(0, q, b)
            if q == 4:
                re.append(yr * cosine if b else yr)
                im.append(yr * -sine if b else jnp.zeros_like(yr))
            else:
                yi = part(1, q, b)
                re.append(yr * cosine + yi * sine if b else yr)
                im.append(yi * cosine - yr * sine if b else yi)
        z = complex8(re, im)
        for r in range(4 if q == 4 else 8):
            turn(slot, *z[r])
            slot += 1


def inner_transform(last_ref, turned_ref, spec_ref):
    left = turned_ref[...]
    high = left.astype(jnp.bfloat16)
    low = (left - high.astype(jnp.float32)).astype(jnp.bfloat16)
    spec_ref[...] = jnp.dot(
        jnp.concatenate([high, low, high], axis=1), last_ref[...], preferred_element_type=jnp.float32
    )


def level_rows(spec_ref, out_ref, turn_ref, first):
    bf16 = jnp.bfloat16
    lane = lax.broadcasted_iota(jnp.int32, (PART, LANES), 1)

    for lanes in (pl.ds(0, LANES), pl.ds(LANES, LANES)):
        whole, moved = spec_ref[pl.ds(first, PART), lanes], spec_ref[pl.ds(ROWS + first, PART), lanes]
        whole = jnp.where(lane == 0, pltpu.roll(whole, 96, 1), whole)
        spec_ref[pl.ds(ROWS + first, PART), lanes] = jnp.where(lane % 64 < 32, whole, moved)

    def get(slot):
        rows = pl.ds((slot + 1) * ROWS + first, PART)
        return spec_ref[rows, pl.ds(0, LANES)], spec_ref[rows, pl.ds(LANES, LANES)]

    total = None
    for slot in range(SLOTS):
        re, im = get(slot)
        power = re * re + im * im
        if slot == 0:
            power = jnp.where(lane == 64, power * 0.5, power)
        total = power if total is None else total + power
    level = jnp.sum(total, axis=-1, keepdims=True) * (2.0 / NF)
    floor = jnp.broadcast_to(0.1 * level + 1e-06, (PART, LANES))
    for slot in range(SLOTS):
        re, im = get(slot)
        scale = lax.rsqrt(re * re + im * im + floor)
        turn_ref[pl.ds(first * TURN + slot, PART, stride=TURN), :] = re * scale
        turn_ref[pl.ds(first * TURN + slot + SLOTS, PART, stride=TURN), :] = im * scale
    for r in range(PART):
        out_ref[r // 16, r % 16] = turn_ref[pl.ds((first + r) * TURN, 2 * SLOTS), :].astype(bf16)


def whiten_kernel(
    raw_hbm, twist_hbm, last_hbm, out_hbm, raw_ref, twist_ref, last_ref, out_ref, in_sem, table_sem, out_sem, *work
):
    def fetch(g):
        return pltpu.make_async_copy(raw_hbm.at[0, pl.ds(g * ROWS, ROWS)], raw_ref.at[g], in_sem.at[g])

    def leave(g, j):
        return pltpu.make_async_copy(out_ref.at[g, j], out_hbm.at[:, :, g, j], out_sem.at[g, j])

    twist = pltpu.make_async_copy(twist_hbm, twist_ref, table_sem.at[0])
    last = pltpu.make_async_copy(last_hbm, last_ref, table_sem.at[1])
    fetch(0).start()
    twist.start()
    last.start()
    for g in range(1, STEPS):
        fetch(g).start()
    part, turned, spec, turn = work

    def outer(g):
        outer_transform(raw_ref.at[g], twist_ref, turned, part)

    twist.wait()
    fetch(0).wait()
    outer(0)
    last.wait()

    def level(g):
        for j in range(2):
            level_rows(spec, out_ref.at[g, j], turn, j * PART)
            leave(g, j).start()

    fetch(1).wait()
    inner_transform(last_ref, turned, spec)
    outer(1)
    level(0)
    inner_transform(last_ref, turned, spec)
    level(1)
    for g in range(STEPS):
        for j in range(2):
            leave(g, j).wait()


def whiten(raw):
    far = pl.BlockSpec(memory_space=pltpu.HBM)
    return pl.pallas_call(
        whiten_kernel,
        out_shape=jax.ShapeDtypeStruct((2, 16, 2, 2, 2 * SLOTS, LANES), jnp.bfloat16),
        in_specs=[far] * 3,
        out_specs=far,
        scratch_shapes=[
            pltpu.VMEM((STEPS, ROWS, NF), jnp.bfloat16),
            pltpu.VMEM((2, SLOTS, LANES), jnp.float32),
            pltpu.VMEM((6 * LANES, 2 * LANES), jnp.bfloat16),
            pltpu.VMEM((STEPS, 2, 2, 16, 2 * SLOTS, LANES), jnp.bfloat16),
            pltpu.SemaphoreType.DMA((STEPS,)),
            pltpu.SemaphoreType.DMA((2,)),
            pltpu.SemaphoreType.DMA((STEPS, 2)),
            pltpu.VMEM((2, 5, 8, ROWS, LANES), jnp.float32),
            pltpu.VMEM(((SLOTS + 1) * ROWS, 2 * LANES), jnp.float32),
            pltpu.VMEM(((SLOTS + 1) * ROWS, 2 * LANES), jnp.float32),
            pltpu.VMEM((ROWS * TURN + TURN, LANES), jnp.float32),
        ],
        compiler_params=pltpu.CompilerParams(vmem_limit_bytes=60 * 2**20),
        name="whiten",
    )(raw, jnp.asarray(twiddles()), jnp.asarray(last_transform()))


def lag_kernel(
    pairs_ref, spec_ref, table_hbm, keep_ref, send_ref, cross_ref, left_ref, table_ref, turn_ref, table_sem
):
    f32, bf16 = jnp.float32, jnp.bfloat16
    depth = table_ref.shape[1]
    half = SLOTS // 2

    def fetch(c):
        return pltpu.make_async_copy(table_hbm.at[c], table_ref.at[c], table_sem.at[c])

    for c in range(2 * CHUNKS):
        fetch(c).start()

    lower = lax.broadcasted_iota(jnp.int32, (half, LANES), 1) < 64

    def one(i, carry):
        pair = pairs_ref[pl.ds(i, 1), :]
        first, second = pair[0, 0], pair[0, 1]
        for h in range(2):
            for j in range(2):
                a = spec_ref[h * 32 + first, j].astype(f32)
                b = spec_ref[h * 32 + second, j].astype(f32)
                ar, ai, br, bi = a[:SLOTS], a[SLOTS:], b[:SLOTS], b[SLOTS:]
                row = pl.multiple_of(((h * 2 + j) * 32 + i) * TURN, 8)
                for part, cross in ((0, ar * br + ai * bi), (1, ai * br - ar * bi)):
                    near = jnp.where(lower, cross[:half], cross[half:])
                    away = pltpu.roll(jnp.where(lower, cross[half:], cross[:half]), 64, 1)
                    cross_ref[pl.ds(row + part * half, half), :] = near
                    cross_ref[pl.ds(row + (2 + part) * half, half), :] = away
        return carry

    lax.fori_loop(0, 32, one, 0, unroll=8)
    lane = lax.broadcasted_iota(jnp.int32, (128, LANES), 1)
    cosines = far_cosines()
    far, middle = None, None
    for side in range(2):
        for slot in range(SLOTS):
            cross = cross_ref[pl.ds(side * SLOTS + slot, 128, stride=TURN), :].astype(bf16)
            term = cross.astype(f32) if slot < half else None
            if side == 1 and slot % half == 0:
                if slot == 0:
                    middle = 0.5 * term[:, :1]
                    term = jnp.where(lane == 0, 0.0, term)
                cross = jnp.where(lane == 0, jnp.zeros_like(cross), cross)
            left_ref[pl.ds(side * 128, 128), pl.ds(slot * LANES, LANES)] = cross
            if slot < half:
                term = term * jnp.where(lane < 64, *cosines[slot])
                far = term if far is None else far + term
    far = jnp.sum(far, axis=-1, keepdims=True) + middle
    far, middle = far[:64] + far[64:], middle[:64] + middle[64:]

    for c in range(2 * CHUNKS):
        fetch(c).wait()
    sums = []
    for part in range(2):
        total = None
        for c in range(part * CHUNKS, (part + 1) * CHUNKS):
            left = left_ref[:, pl.ds(c * depth, depth)]
            term = jnp.dot(left, table_ref[c], preferred_element_type=f32)
            total = term if total is None else total + term
        near, away = total[:64] + total[64:128], total[128:192] + total[192:]
        sums.append((near[:, :256] + away[:, :256], near[:, 256:] - away[:, 256:]))
    (even_cosine, odd_cosine), (even_sine, odd_sine) = sums
    even_cosine, odd_cosine = even_cosine + middle, odd_cosine - middle
    lane = lax.broadcasted_iota(jnp.int32, (64, LANES), 1)
    for q in range(2):
        run = slice(q * LANES, (q + 1) * LANES)
        c, s = even_cosine[:, run], even_sine[:, run]
        minus, plus = c + s, c - s
        if q == 0:
            minus, plus = jnp.where(lane == 0, far + s, minus), jnp.where(lane == 0, c, plus)
        c, s = odd_cosine[:, run], odd_sine[:, run]
        for place, lags in ((q, minus), (q + 2, c + s), (q + 4, plus), (q + 6, c - s)):
            turn_ref[pl.ds(place, 64, stride=8), :] = lags * (2.0 * NF**-0.5)
    turned = turn_ref[pl.ds(0, 64 * 8), :].reshape(2, 2, 16, 8, LANES)
    keep_ref[...] = turned[:, 0].astype(bf16)
    send_ref[...] = turned[:, 1].astype(bf16)


def correlate(pairs, spectra):
    half = jax.ShapeDtypeStruct((2, 16, 8, LANES), jnp.bfloat16)
    vmem = pl.BlockSpec(memory_space=pltpu.VMEM)
    tables = pltpu.with_memory_space_constraint(jnp.asarray(lag_tables()), pltpu.HBM)
    return pl.pallas_call(
        lag_kernel,
        out_shape=(half, half),
        in_specs=[vmem, vmem, pl.BlockSpec(memory_space=pltpu.HBM)],
        out_specs=(vmem, vmem),
        scratch_shapes=[
            pltpu.VMEM((128 * TURN + TURN, LANES), jnp.float32),
            pltpu.VMEM((256, NF // 2), jnp.bfloat16),
            pltpu.VMEM(tables.shape, jnp.bfloat16),
            pltpu.VMEM((64 * 8 + 8, LANES), jnp.float32),
            pltpu.SemaphoreType.DMA((2 * CHUNKS,)),
        ],
        compiler_params=pltpu.CompilerParams(vmem_limit_bytes=24 * 2**20),
        name="correlate",
    )(pairs, spectra, tables)


def stack_kernel(lags_ref, out_ref, turn_ref):
    total = lags_ref[0].astype(jnp.float32)
    for t in range(1, 4):
        total = total + lags_ref[t].astype(jnp.float32)
    turn_ref[pl.ds(0, 16 * 8), :] = total.reshape(16 * 8, LANES)
    runs = [turn_ref[pl.ds(q, 16, stride=8), :] for q in range(8)]
    lane = lax.broadcasted_iota(jnp.int32, (16, LANES), 1)

    def pick(run, index):
        return jnp.take_along_axis(run, index, axis=1, mode="promise_in_bounds")

    for q in range(4):
        index = 64 * (q % 2) + lane // 2
        even, odd = pick(runs[4 + q // 2], index), pick(runs[6 + q // 2], index)
        out_ref[0, :, pl.ds((4 + q) * LANES, LANES)] = jnp.where(lane % 2 == 0, even, odd)
    for q in range(4):
        b, after = 3 - q, (4 - q) % 4
        even = pick(runs[b // 2], 64 * (b % 2) + (64 - lane // 2) % 64)
        first = pick(runs[after // 2], jnp.full_like(lane, 64 * (after % 2)))
        odd = pick(runs[2 + b // 2], 64 * (b % 2) + 63 - lane // 2)
        even = jnp.where(lane == 0, first, even)
        out_ref[0, :, pl.ds(q * LANES, LANES)] = jnp.where(lane % 2 == 0, even, odd)


def stack(lags):
    vmem = pl.BlockSpec(memory_space=pltpu.VMEM)
    return pl.pallas_call(
        stack_kernel,
        out_shape=jax.ShapeDtypeStruct((1, 16, LAGS), jnp.float32),
        in_specs=[vmem],
        out_specs=vmem,
        scratch_shapes=[pltpu.VMEM((16 * 8 + 8, LANES), jnp.float32)],
        name="stack",
    )(lags)


def body(raw, pair_blocks):
    core = lax.axis_index("blk") % 2
    near = [[32 * (2 * t + h) + d for h in range(2) for d in range(32)] for t in range(4)]
    far = [
        [32 * (2 * t + h) + 2 * chip + c for t in range(4) for chip in range(16)]
        for h in range(2)
        for c in range(2)
    ]
    spectra = whiten(raw).reshape(64, 2 * 2 * SLOTS, LANES)
    spectra = lax.all_to_all(spectra, AXES, 0, 0, axis_index_groups=near, tiled=True)
    spectra = spectra.reshape(64, 2, 2 * SLOTS, LANES)
    order = pair_blocks.reshape(16, 2, 2)
    order = jnp.where(core == 0, order, order[:, ::-1]).transpose(1, 0, 2).reshape(32, 2)
    order = jnp.pad(order, ((0, 0), (0, LANES - 2)))
    keep, send = correlate(order, spectra)
    got = lax.ppermute(send, "blk", [(i, i ^ 1) for i in range(32)])
    lags = jnp.where(core == 0, jnp.stack([keep, got]), jnp.stack([got, keep]))
    lags = lax.all_to_all(lags.reshape(64, 8, LANES), AXES, 0, 0, axis_index_groups=far, tiled=True)
    return stack(pltpu.with_memory_space_constraint(lags.reshape(4, 16, 8, LANES), pltpu.VMEM))


def solution(mesh):
    in_specs = (P("section", "blk", None), P())
    out_specs = P("blk", "section", None)
    return jax.shard_map(body, mesh=mesh, in_specs=in_specs, out_specs=out_specs, check_vma=False)
```

```python
import math

import jax
import jax.numpy as jnp
import ml_dtypes
import numpy as np
from jax import lax
from jax.experimental import pallas as pl
from jax.experimental.pallas import tpu as pltpu
from jax.sharding import PartitionSpec as P

NF = 8192
LAGS = 1024
LANES = 128
ROWS = 64
STEPS = 2
PART = 32
PIECES = 2
SLOTS = 32
TURN = 72
CHUNKS = 4
HALF = math.sqrt(0.5)
AXES = ("section", "blk")
RESIDUES = (
    [8, 16, 24]
    + [4 + 8 * r for r in range(4)]
    + [q + 8 * r for q in (1, 2, 3) for r in range(8)]
)


def bin_numbers():
    lane = np.arange(LANES)
    first = np.where(lane % 64 < 32, 64 * lane, 32 + 64 * (lane - 32))
    first[0] = 2048
    return np.stack([first] + [r + 64 * lane for r in RESIDUES])


def twiddles():
    lane = np.arange(LANES)
    turns = [lane / 256.0 - lane / 4.0] + [lane * r / NF for r in RESIDUES]
    angle = 2.0 * np.pi * np.stack(turns)
    return np.stack([np.cos(angle), np.sin(angle)]).astype(np.float32)


def last_transform():
    index = np.arange(LANES)
    angle = 2.0 * np.pi * (index[:, None] * index[None, :] % LANES) / LANES
    cosine, sine = np.cos(angle), np.sin(angle)
    full = np.block([[cosine, -sine], [sine, cosine]])
    high = full.astype(ml_dtypes.bfloat16)
    low = (full - high.astype(np.float64)).astype(ml_dtypes.bfloat16)
    return np.concatenate([high, high, low])


def folded_bins():
    bins = bin_numbers()
    return np.concatenate([bins[:16, :64], bins[16:, :64]], axis=1)


def folded_bins():
    bins = bin_numbers()
    return np.concatenate([bins[:16, :64], bins[16:, :64]], axis=1)


def lag_tables():
    bins = folded_bins().reshape(-1)[:, None]
    even, odd = 2 * np.arange(256)[None, :], 2 * np.arange(256)[None, :] + 1
    sign = np.where(np.arange(LANES) < 64, 1.0, -1.0)[None, :, None]
    tables = []
    for function, first in ((np.cos, 0), (np.sin, 512)):
        near = function(2.0 * np.pi * (bins * np.where(even == 0, first, even) % NF) / NF)
        far = function(2.0 * np.pi * (bins * odd % NF) / NF).reshape(16, LANES, 256) * sign
        tables.append(np.concatenate([near, far.reshape(-1, 256)], axis=1))
    return np.stack(tables).astype(ml_dtypes.bfloat16).reshape(2 * CHUNKS, -1, 512)


def far_cosines():
    bins = folded_bins()[:, [1, LANES - 1]]
    cosines = np.cos(2.0 * np.pi * (bins * 512 % NF) / NF).astype(ml_dtypes.bfloat16)
    return [(float(low), float(high)) for low, high in cosines]


def real8(x):
    s0, d0, s2, d2 = x[0] + x[4], x[0] - x[4], x[2] + x[6], x[2] - x[6]
    s1, d1, s3, d3 = x[1] + x[5], x[1] - x[5], x[3] + x[7], x[3] - x[7]
    even, odd = s0 + s2, s1 + s3
    u, v = (d1 - d3) * HALF, (d1 + d3) * HALF
    return [
        (even + odd, None),
        (d0 + u, -(d2 + v)),
        (s0 - s2, s3 - s1),
        (d0 - u, d2 - v),
        (even - odd, None),
    ]


def complex8(re, im):
    def add(i, j):
        return (i[0] + j[0], i[1] + j[1])

    def sub(i, j):
        return (i[0] - j[0], i[1] - j[1])

    def sub_i(i, j):
        return (i[0] + j[1], i[1] - j[0])

    def add_i(i, j):
        return (i[0] - j[1], i[1] + j[0])

    t = list(zip(re, im))
    a0, a1, a2, a3 = add(t[0], t[4]), sub(t[0], t[4]), add(t[2], t[6]), sub(t[2], t[6])
    a4, a5, a6, a7 = add(t[1], t[5]), sub(t[1], t[5]), add(t[3], t[7]), sub(t[3], t[7])
    b0, b2, b1, b3 = add(a0, a2), sub(a0, a2), sub_i(a1, a3), add_i(a1, a3)
    b4, b6, b5, b7 = add(a4, a6), sub(a4, a6), sub_i(a5, a7), add_i(a5, a7)
    c5 = ((b5[0] + b5[1]) * HALF, (b5[1] - b5[0]) * HALF)
    c7 = ((b7[1] - b7[0]) * HALF, (b7[0] + b7[1]) * -HALF)
    return [
        add(b0, b4), add(b1, c5), sub_i(b2, b6), add(b3, c7),
        sub(b0, b4), sub(b1, c5), add_i(b2, b6), sub(b3, c7),
    ]


def outer_transform(raw_ref, twist_ref, turned_ref, part_ref):
    f32 = jnp.float32
    for first in range(0, ROWS, 32):
        rows = pl.ds(first, 32)
        for b in range(8):
            x = [raw_ref[rows, pl.ds((8 * a + b) * LANES, LANES)].astype(f32) for a in range(8)]
            y = real8(x)
            for q in range(5):
                part_ref[0, q, b, rows] = y[q][0]
                if y[q][1] is not None:
                    part_ref[1, q, b, rows] = y[q][1]
    for first in range(0, ROWS, 8):
        second_transform(first, 8, twist_ref, turned_ref, part_ref)


def second_transform(first, count, twist_ref, turned_ref, part_ref):
    def put(slot, re, im):
        rows = pl.ds(slot * ROWS + first, count)
        turned_ref[rows, pl.ds(0, LANES)] = re
        turned_ref[rows, pl.ds(LANES, LANES)] = im

    def turn(slot, re, im):
        cosine, sine = twist_ref[0, slot - 1 : slot, :], twist_ref[1, slot - 1 : slot, :]
        if im is None:
            put(slot, re * cosine, re * -sine)
        else:
            put(slot, re * cosine + im * sine, im * cosine - re * sine)

    def part(side, q, b):
        return part_ref[side, q, b, pl.ds(first, count)]

    whole = real8([part(0, 0, b) for b in range(8)])
    zero = whole[0][0]
    put(0, zero - jnp.mean(zero, axis=-1, keepdims=True), jnp.zeros_like(zero))
    turn(1, whole[4][0], None)
    for r in (1, 2, 3):
        turn(1 + r, *whole[r])
    slot = 5
    for q in (4, 1, 2, 3):
        re, im = [], []
        for b in range(8):
            cosine, sine = math.cos(2 * math.pi * b * q / 64), math.sin(2 * math.pi * b * q / 64)
            yr = part(0, q, b)
            if q == 4:
                re.append(yr * cosine if b else yr)
                im.append(yr * -sine if b else jnp.zeros_like(yr))
            else:
                yi = part(1, q, b)
                re.append(yr * cosine + yi * sine if b else yr)
                im.append(yi * cosine - yr * sine if b else yi)
        z = complex8(re, im)
        for r in range(4 if q == 4 else 8):
            turn(slot, *z[r])
            slot += 1


def inner_transform(last_ref, turned_ref, spec_ref):
    left = turned_ref[...]
    high = left.astype(jnp.bfloat16)
    low = (left - high.astype(jnp.float32)).astype(jnp.bfloat16)
    spec_ref[...] = jnp.dot(
        jnp.concatenate([high, low, high], axis=1), last_ref[...], preferred_element_type=jnp.float32
    )


def level_rows(spec_ref, out_ref, turn_ref, first):
    bf16 = jnp.bfloat16
    lane = lax.broadcasted_iota(jnp.int32, (PART, LANES), 1)

    for lanes in (pl.ds(0, LANES), pl.ds(LANES, LANES)):
        whole, moved = spec_ref[pl.ds(first, PART), lanes], spec_ref[pl.ds(ROWS + first, PART), lanes]
        whole = jnp.where(lane == 0, pltpu.roll(whole, 96, 1), whole)
        spec_ref[pl.ds(ROWS + first, PART), lanes] = jnp.where(lane % 64 < 32, whole, moved)

    def get(slot):
        rows = pl.ds((slot + 1) * ROWS + first, PART)
        return spec_ref[rows, pl.ds(0, LANES)], spec_ref[rows, pl.ds(LANES, LANES)]

    total = None
    for slot in range(SLOTS):
        re, im = get(slot)
        power = re * re + im * im
        if slot == 0:
            power = jnp.where(lane == 64, power * 0.5, power)
        total = power if total is None else total + power
    level = jnp.sum(total, axis=-1, keepdims=True) * (2.0 / NF)
    floor = jnp.broadcast_to(0.1 * level + 1e-06, (PART, LANES))
    for slot in range(SLOTS):
        re, im = get(slot)
        scale = lax.rsqrt(re * re + im * im + floor)
        turn_ref[pl.ds(first * TURN + slot, PART, stride=TURN), :] = re * scale
        turn_ref[pl.ds(first * TURN + slot + SLOTS, PART, stride=TURN), :] = im * scale
    for r in range(PART):
        out_ref[r // 16, r % 16] = turn_ref[pl.ds((first + r) * TURN, 2 * SLOTS), :].astype(bf16)


def whiten_kernel(
    raw_hbm, twist_hbm, last_hbm, out_hbm, raw_ref, twist_ref, last_ref, out_ref, in_sem, table_sem, out_sem, *work
):
    def fetch(g, part):
        rows = pl.ds(part * 32, 32)
        source = raw_hbm.at[0, pl.ds(g * ROWS + part * 32, 32)]
        return pltpu.make_async_copy(source, raw_ref.at[g, rows], in_sem.at[g, part])

    def leave(g, j):
        return pltpu.make_async_copy(out_ref.at[g, j], out_hbm.at[:, :, g, j], out_sem.at[g, j])

    twist = pltpu.make_async_copy(twist_hbm, twist_ref, table_sem.at[0])
    last = pltpu.make_async_copy(last_hbm, last_ref, table_sem.at[1])
    for p in range(PIECES):
        fetch(0, p).start()
    twist.start()
    last.start()
    for p in range(PIECES):
        fetch(1, p).start()
    part, turned, spec, turn = work

    def outer(g):
        outer_transform(raw_ref.at[g], twist_ref, turned, part)

    twist.wait()
    for p in range(PIECES):
        fetch(0, p).wait()
    outer(0)
    last.wait()

    def level(g):
        for j in range(2):
            level_rows(spec, out_ref.at[g, j], turn, j * PART)
            leave(g, j).start()

    for p in range(PIECES):
        fetch(1, p).wait()
    inner_transform(last_ref, turned, spec)
    outer(1)
    level(0)
    inner_transform(last_ref, turned, spec)
    level(1)
    for g in range(STEPS):
        for j in range(2):
            leave(g, j).wait()


def whiten(raw):
    far = pl.BlockSpec(memory_space=pltpu.HBM)
    return pl.pallas_call(
        whiten_kernel,
        out_shape=jax.ShapeDtypeStruct((2, 16, 2, 2, 2 * SLOTS, LANES), jnp.bfloat16),
        in_specs=[far] * 3,
        out_specs=far,
        scratch_shapes=[
            pltpu.VMEM((STEPS, ROWS, NF), jnp.bfloat16),
            pltpu.VMEM((2, SLOTS, LANES), jnp.float32),
            pltpu.VMEM((6 * LANES, 2 * LANES), jnp.bfloat16),
            pltpu.VMEM((STEPS, 2, 2, 16, 2 * SLOTS, LANES), jnp.bfloat16),
            pltpu.SemaphoreType.DMA((STEPS, PIECES)),
            pltpu.SemaphoreType.DMA((2,)),
            pltpu.SemaphoreType.DMA((STEPS, 2)),
            pltpu.VMEM((2, 5, 8, ROWS, LANES), jnp.float32),
            pltpu.VMEM(((SLOTS + 1) * ROWS, 2 * LANES), jnp.float32),
            pltpu.VMEM(((SLOTS + 1) * ROWS, 2 * LANES), jnp.float32),
            pltpu.VMEM((ROWS * TURN + TURN, LANES), jnp.float32),
        ],
        compiler_params=pltpu.CompilerParams(vmem_limit_bytes=60 * 2**20),
        name="whiten",
    )(raw, jnp.asarray(twiddles()), jnp.asarray(last_transform()))


def lag_kernel(
    pairs_ref, spec_ref, table_hbm, keep_ref, send_ref, cross_ref, left_ref, table_ref, turn_ref, table_sem
):
    f32, bf16 = jnp.float32, jnp.bfloat16
    depth = table_ref.shape[1]
    half = SLOTS // 2

    def fetch(c):
        return pltpu.make_async_copy(table_hbm.at[c], table_ref.at[c], table_sem.at[c])

    for c in range(2 * CHUNKS):
        fetch(c).start()

    lower = lax.broadcasted_iota(jnp.int32, (half, LANES), 1) < 64

    def one(i, carry):
        pair = pairs_ref[pl.ds(i, 1), :]
        first, second = pair[0, 0], pair[0, 1]
        for h in range(2):
            for j in range(2):
                a = spec_ref[h * 32 + first, j].astype(f32)
                b = spec_ref[h * 32 + second, j].astype(f32)
                ar, ai, br, bi = a[:SLOTS], a[SLOTS:], b[:SLOTS], b[SLOTS:]
                row = pl.multiple_of(((h * 2 + j) * 32 + i) * TURN, 8)
                for part, cross in ((0, ar * br + ai * bi), (1, ai * br - ar * bi)):
                    near = jnp.where(lower, cross[:half], cross[half:])
                    away = pltpu.roll(jnp.where(lower, cross[half:], cross[:half]), 64, 1)
                    cross_ref[pl.ds(row + part * half, half), :] = near
                    cross_ref[pl.ds(row + (2 + part) * half, half), :] = away
        return carry

    lax.fori_loop(0, 32, one, 0, unroll=8)
    lane = lax.broadcasted_iota(jnp.int32, (128, LANES), 1)
    cosines = far_cosines()
    far, middle = None, None
    for side in range(2):
        for slot in range(SLOTS):
            cross = cross_ref[pl.ds(side * SLOTS + slot, 128, stride=TURN), :].astype(bf16)
            term = cross.astype(f32) if slot < half else None
            if side == 1 and slot % half == 0:
                if slot == 0:
                    middle = 0.5 * term[:, :1]
                    term = jnp.where(lane == 0, 0.0, term)
                cross = jnp.where(lane == 0, jnp.zeros_like(cross), cross)
            left_ref[pl.ds(side * 128, 128), pl.ds(slot * LANES, LANES)] = cross
            if slot < half:
                term = term * jnp.where(lane < 64, *cosines[slot])
                far = term if far is None else far + term
    far = jnp.sum(far, axis=-1, keepdims=True) + middle
    far, middle = far[:64] + far[64:], middle[:64] + middle[64:]

    for c in range(2 * CHUNKS):
        fetch(c).wait()
    sums = []
    for part in range(2):
        total = None
        for c in range(part * CHUNKS, (part + 1) * CHUNKS):
            left = left_ref[:, pl.ds(c * depth, depth)]
            term = jnp.dot(left, table_ref[c], preferred_element_type=f32)
            total = term if total is None else total + term
        near, away = total[:64] + total[64:128], total[128:192] + total[192:]
        sums.append((near[:, :256] + away[:, :256], near[:, 256:] - away[:, 256:]))
    (even_cosine, odd_cosine), (even_sine, odd_sine) = sums
    even_cosine, odd_cosine = even_cosine + middle, odd_cosine - middle
    lane = lax.broadcasted_iota(jnp.int32, (64, LANES), 1)
    for q in range(2):
        run = slice(q * LANES, (q + 1) * LANES)
        c, s = even_cosine[:, run], even_sine[:, run]
        minus, plus = c + s, c - s
        if q == 0:
            minus, plus = jnp.where(lane == 0, far + s, minus), jnp.where(lane == 0, c, plus)
        c, s = odd_cosine[:, run], odd_sine[:, run]
        for place, lags in ((q, minus), (q + 2, c + s), (q + 4, plus), (q + 6, c - s)):
            turn_ref[pl.ds(place, 64, stride=8), :] = lags * (2.0 * NF**-0.5)
    turned = turn_ref[pl.ds(0, 64 * 8), :].reshape(2, 2, 16, 8, LANES)
    keep_ref[...] = turned[:, 0].astype(bf16)
    send_ref[...] = turned[:, 1].astype(bf16)


def correlate(pairs, spectra):
    half = jax.ShapeDtypeStruct((2, 16, 8, LANES), jnp.bfloat16)
    vmem = pl.BlockSpec(memory_space=pltpu.VMEM)
    tables = pltpu.with_memory_space_constraint(jnp.asarray(lag_tables()), pltpu.HBM)
    return pl.pallas_call(
        lag_kernel,
        out_shape=(half, half),
        in_specs=[vmem, vmem, pl.BlockSpec(memory_space=pltpu.HBM)],
        out_specs=(vmem, vmem),
        scratch_shapes=[
            pltpu.VMEM((128 * TURN + TURN, LANES), jnp.float32),
            pltpu.VMEM((256, NF // 2), jnp.bfloat16),
            pltpu.VMEM(tables.shape, jnp.bfloat16),
            pltpu.VMEM((64 * 8 + 8, LANES), jnp.float32),
            pltpu.SemaphoreType.DMA((2 * CHUNKS,)),
        ],
        compiler_params=pltpu.CompilerParams(vmem_limit_bytes=24 * 2**20),
        name="correlate",
    )(pairs, spectra, tables)


def stack_kernel(lags_ref, out_ref, turn_ref):
    total = lags_ref[0].astype(jnp.float32)
    for t in range(1, 4):
        total = total + lags_ref[t].astype(jnp.float32)
    turn_ref[pl.ds(0, 16 * 8), :] = total.reshape(16 * 8, LANES)
    runs = [turn_ref[pl.ds(q, 16, stride=8), :] for q in range(8)]
    lane = lax.broadcasted_iota(jnp.int32, (16, LANES), 1)

    def pick(run, index):
        return jnp.take_along_axis(run, index, axis=1, mode="promise_in_bounds")

    for q in range(4):
        index = 64 * (q % 2) + lane // 2
        even, odd = pick(runs[4 + q // 2], index), pick(runs[6 + q // 2], index)
        out_ref[0, :, pl.ds((4 + q) * LANES, LANES)] = jnp.where(lane % 2 == 0, even, odd)
    for q in range(4):
        b, after = 3 - q, (4 - q) % 4
        even = pick(runs[b // 2], 64 * (b % 2) + (64 - lane // 2) % 64)
        first = pick(runs[after // 2], jnp.full_like(lane, 64 * (after % 2)))
        odd = pick(runs[2 + b // 2], 64 * (b % 2) + 63 - lane // 2)
        even = jnp.where(lane == 0, first, even)
        out_ref[0, :, pl.ds(q * LANES, LANES)] = jnp.where(lane % 2 == 0, even, odd)


def stack(lags):
    vmem = pl.BlockSpec(memory_space=pltpu.VMEM)
    return pl.pallas_call(
        stack_kernel,
        out_shape=jax.ShapeDtypeStruct((1, 16, LAGS), jnp.float32),
        in_specs=[vmem],
        out_specs=vmem,
        scratch_shapes=[pltpu.VMEM((16 * 8 + 8, LANES), jnp.float32)],
        name="stack",
    )(lags)


def body(raw, pair_blocks):
    core = lax.axis_index("blk") % 2
    near = [[32 * (2 * t + h) + d for h in range(2) for d in range(32)] for t in range(4)]
    far = [
        [32 * (2 * t + h) + 2 * chip + c for t in range(4) for chip in range(16)]
        for h in range(2)
        for c in range(2)
    ]
    spectra = whiten(raw).reshape(64, 2 * 2 * SLOTS, LANES)
    spectra = lax.all_to_all(spectra, AXES, 0, 0, axis_index_groups=near, tiled=True)
    spectra = spectra.reshape(64, 2, 2 * SLOTS, LANES)
    order = pair_blocks.reshape(16, 2, 2)
    order = jnp.where(core == 0, order, order[:, ::-1]).transpose(1, 0, 2).reshape(32, 2)
    order = jnp.pad(order, ((0, 0), (0, LANES - 2)))
    keep, send = correlate(order, spectra)
    got = lax.ppermute(send, "blk", [(i, i ^ 1) for i in range(32)])
    lags = jnp.where(core == 0, jnp.stack([keep, got]), jnp.stack([got, keep]))
    lags = lax.all_to_all(lags.reshape(64, 8, LANES), AXES, 0, 0, axis_index_groups=far, tiled=True)
    return stack(pltpu.with_memory_space_constraint(lags.reshape(4, 16, 8, LANES), pltpu.VMEM))


def solution(mesh):
    in_specs = (P("section", "blk", None), P())
    out_specs = P("blk", "section", None)
    return jax.shard_map(body, mesh=mesh, in_specs=in_specs, out_specs=out_specs, check_vma=False)
```
